32 devices in a mesh: group: 2 (over x), chan: 8 (over z, y), tm: 2 (over core).
Axes of the slice: x: 2, y: 2, z: 4, core: 2. Of those that a mesh axis runs over, the one named last changes fastest.
Arguments:
- signal: float32 [1664, 16384], P(('group', 'chan'), 'tm'), parts along dimension 0, may hold values from -56 to 56
- valid_flags: int32 [1664, 16], P(('group', 'chan'), 'tm'), parts along dimension 0, may hold values 0 or 1
Outputs:
- correlations: bfloat16 [2, 104, 1664, 512], P(None, 'tm', ('group', 'chan')), parts along dimension 2
The draws below stay inside these ranges and needn't reach their ends.
There are 2 independent parts, one for each index of `group`. The reference program is written for one: setup_inputs(seed, part) draws one part's arguments, and reference() takes and returns one part's arrays. A program takes and returns all parts, laid end to end along the dimension named above; each array names one. Nothing has to cross between parts.
All inputs are finite; a program needn't handle non-finite values. No bound on the sum of `valid_flags` on one device may be relied on, other than what follows from the above.
Results may differ from the reference program's by a relative error of at most 0.009.
Values may be sent and summed in bfloat16 or wider, within the bound.
A program may use at most 192 MiB of HBM per device.

```python
import jax
import jax.numpy as jnp
from jax import lax

BLOCK = 104
WIN_DEV = 8
WINDOW = 1024
LAGS = 512
ROUNDS = 2
CHANNELS = 832
WINDOWS = 16
SAMPLES = 16384
N_CHAN = 8
N_TM = 2


def draw_signal(key, part):
    key_one, key_two, key_three, key_four = jax.random.split(key, 4)
    padded_length = SAMPLES + CHANNELS
    forward_wave = jax.random.truncated_normal(key_one, -4.0, 4.0, (padded_length,), jnp.float32)
    backward_wave = jax.random.truncated_normal(key_two, -4.0, 4.0, (padded_length,), jnp.float32)
    local_noise = jax.random.truncated_normal(key_three, -4.0, 4.0, (CHANNELS, SAMPLES), jnp.float32)
    window_gains = jnp.exp(jax.random.uniform(key_four, (CHANNELS, WINDOWS), jnp.float32, 0.0, 2.302585))

    def one_channel(channel_index):
        delay = channel_index // 2
        ahead_part = lax.dynamic_slice_in_dim(forward_wave, CHANNELS - delay, SAMPLES)
        behind = lax.dynamic_slice_in_dim(backward_wave, delay, SAMPLES)
        return ahead_part + behind
    coherent = lax.map(one_channel, jnp.arange(CHANNELS, dtype=jnp.int32))
    combined = 0.2 * coherent + local_noise
    scaled = combined.reshape(CHANNELS, WINDOWS, WINDOW) * window_gains[:, :, None]
    return scaled.reshape(CHANNELS, SAMPLES)


def plant(entries, own_key, least, high):
    dims = entries.shape
    spot = [jax.random.randint(jax.random.fold_in(own_key, axis), (), 0, dims[axis]) for axis in range(len(dims))]
    entries = entries.at[tuple(spot)].set(least)
    longest = dims.index(max(dims))
    spot[longest] = (spot[longest] + 1) % dims[longest]
    return entries.at[tuple(spot)].set(high)


def setup_inputs(seed: int = 0, part: int = 0) -> dict:
    streams_of = jax.random.split(jax.random.key(seed), 3)
    part_keys = jax.random.split(jax.random.fold_in(streams_of[2], part), 3)
    return {
        "signal": draw_signal(jax.random.fold_in(jax.random.fold_in(streams_of[2], part), 71), part),
        "valid_flags": plant((jax.random.randint(part_keys[1], (CHANNELS, WINDOWS), 0, 4) < 3).astype(jnp.int32), jax.random.fold_in(part_keys[1], 1), 0, 1),
    }


epsilon = 1e-06

def taper_table(window):
    sample_axis = jnp.arange(window, dtype=jnp.float32)
    return 0.5 - 0.5 * jnp.cos(2.0 * jnp.pi * sample_axis / window)

def forward_table(window):
    bin_count = window // 2
    sample_index = jnp.arange(window, dtype=jnp.int32)[:, None]
    frequency = jnp.arange(bin_count, dtype=jnp.int32)[None, :]
    phases = 2.0 * jnp.pi / window * (sample_index * frequency % window).astype(jnp.float32)
    return jnp.concatenate([jnp.cos(phases), -jnp.sin(phases)], axis=1).astype(jnp.bfloat16)

def lag_table(window, lag_count, windows):
    bin_count = window // 2
    frequency = jnp.arange(bin_count, dtype=jnp.int32)[:, None]
    shifts = jnp.arange(lag_count, dtype=jnp.int32)[None, :] - lag_count // 2
    phases = 2.0 * jnp.pi / window * (frequency * shifts % window).astype(jnp.float32)
    weight = jnp.where(frequency == 0, 1.0, 2.0).astype(jnp.float32) / (window * float(window * windows) ** 0.5)
    return jnp.concatenate([weight * jnp.cos(phases), -weight * jnp.sin(phases)], axis=0).astype(jnp.bfloat16)

def block_spectra(signal, valid_flags, window):
    row_count = signal.shape[0]
    window_count = signal.shape[1] // window
    pieces = signal.reshape(row_count, window_count, window).astype(jnp.float32)
    mean_square = lax.optimization_barrier(jnp.mean(pieces * pieces, axis=2, keepdims=True))
    tapered = (pieces * lax.rsqrt(mean_square + epsilon) * taper_table(window)).astype(jnp.bfloat16)
    spectra = jnp.dot(tapered.reshape(row_count * window_count, window), forward_table(window), preferred_element_type=jnp.float32)
    spectra = spectra.reshape(row_count, window_count, window) * valid_flags[:, :, None].astype(jnp.float32)
    return spectra.astype(jnp.bfloat16)

def cross_tile(partner, own_spectra):
    bin_count = partner.shape[2] // 2
    rotated = jnp.concatenate([-partner[:, :, bin_count:], partner[:, :, :bin_count]], axis=2)
    paired = jnp.stack([partner, rotated], axis=2).reshape(partner.shape[0], partner.shape[1], 2, 2, bin_count)
    halves = own_spectra.reshape(own_spectra.shape[0], own_spectra.shape[1], 2, bin_count)
    cross = jnp.einsum('dwjkf,cwkf->dcjf', paired.astype(jnp.float32), halves.astype(jnp.float32), precision=lax.Precision.HIGHEST)
    return cross.reshape(partner.shape[0], own_spectra.shape[0], 2 * bin_count)

def reference(signal, valid_flags):

    def spectra_of(pair_in):
        return block_spectra(pair_in[0], pair_in[1], WINDOW)
    spectra = lax.map(spectra_of, (signal.reshape(N_CHAN, BLOCK, SAMPLES), valid_flags.reshape(N_CHAN, BLOCK, WINDOWS)))
    lag_weights = lag_table(WINDOW, LAGS, WINDOWS)

    def one_block(pair_in):
        total = jnp.zeros((BLOCK, BLOCK, WINDOW), jnp.float32)
        for span in range(N_TM):
            partner_part = pair_in[0][:, span * WIN_DEV:(span + 1) * WIN_DEV]
            own_part = pair_in[1][:, span * WIN_DEV:(span + 1) * WIN_DEV]
            total = total + cross_tile(partner_part, own_part).astype(jnp.bfloat16).astype(jnp.float32)
        stacked = total.astype(jnp.bfloat16)
        lagged = jnp.dot(stacked.reshape(BLOCK * BLOCK, WINDOW), lag_weights, preferred_element_type=jnp.float32)
        return lagged.reshape(BLOCK, BLOCK, LAGS).astype(jnp.bfloat16)
    outputs = []
    for round_index in range(ROUNDS):
        partners = jnp.roll(spectra, -(round_index + 1), axis=0)
        tiles = lax.map(one_block, (partners, spectra))
        outputs.append(jnp.transpose(tiles, (1, 0, 2, 3)).reshape(BLOCK, CHANNELS, LAGS))
    return jnp.stack(outputs)
```

```python
import functools

import jax
import jax.numpy as jnp
import numpy as np
from jax import lax
from jax.experimental import pallas as pl
from jax.experimental.pallas import tpu as pltpu
from jax.sharding import PartitionSpec as P

WINDOW = 1024
LAGS = 512
ROUNDS = 2
EPSILON = 1e-06
GROUP = 8
LANES = 128
VMEM_LIMIT = 56 * 1024 * 1024


def taper_table(window):
    t = np.arange(window, dtype=np.float32)
    return (0.5 - 0.5 * np.cos(2.0 * np.pi * t / window)).astype(np.float32)[None, :]


def forward_table(window):
    bins = window // 2
    f = np.arange(bins, dtype=np.int64)[:, None]
    t = np.arange(window, dtype=np.int64)[None, :]
    phases = 2.0 * np.pi / window * (f * t % window)
    table = np.stack([np.cos(phases), -np.sin(phases)])
    table = table.reshape(2, bins // GROUP, GROUP, window).transpose(1, 0, 2, 3)
    return table.reshape(window, window).astype(jnp.bfloat16)


def lag_table(window, lag_count, windows):
    f = np.arange(window // 2, dtype=np.int64)[:, None]
    tau = np.arange(lag_count, dtype=np.int64)[None, :] - lag_count // 2
    phases = 2.0 * np.pi / window * (f * tau % window)
    weight = np.where(f == 0, 1.0, 2.0) / (window * float(window * windows) ** 0.5)
    return np.concatenate([weight * np.cos(phases), -weight * np.sin(phases)]).astype(jnp.bfloat16)


def spectra_kernel(signal_ref, flags_ref, taper_ref, table_ref, out_ref, tapered):
    rows = signal_ref.shape[0]
    windows = flags_ref.shape[1]
    groups = out_ref.shape[0]
    flags = flags_ref[...].astype(jnp.float32)
    tapered[...] = jnp.zeros_like(tapered)
    for w in range(windows):
        piece = signal_ref[:, w * WINDOW : (w + 1) * WINDOW]
        scale = lax.rsqrt(jnp.mean(piece * piece, axis=1, keepdims=True) + EPSILON)
        value = (piece * scale * taper_ref[...]) * flags[:, w : w + 1]
        tapered[w, :rows, :] = value.astype(jnp.bfloat16)
    for pair in range(windows // 2):
        two = tapered[2 * pair : 2 * pair + 2].reshape(2 * LANES, WINDOW)
        value = lax.dot_general(
            table_ref[...], two, (((1,), (1,)), ((), ())), preferred_element_type=jnp.float32
        )
        value = value.reshape(groups, 2, GROUP, 2 * LANES)
        value = jnp.concatenate([value[..., :LANES], value[..., LANES:]], axis=2)
        out_ref[:, :, pair * 2 * GROUP : (pair + 1) * 2 * GROUP, :] = value.astype(jnp.bfloat16)


def cross_kernel(own_ref, other_ref, same_ref, cross_ref, table_ref, *rest, batch):
    out_ref, weights, wide, stacked = rest[-4:]
    count = same_ref.shape[0]
    rows = out_ref.shape[2]
    groups = own_ref.shape[0]
    depth = own_ref.shape[1]
    half = depth // 2
    bins = groups * GROUP
    for place, ref in enumerate((own_ref, other_ref)):
        base = place * depth
        weights[:, base : base + depth, :LANES] = ref[...]
        weights[:, base : base + half, LANES:] = ref[:, half:, :]
        weights[:, base + half : base + depth, LANES:] = -ref[:, :half, :]
    wide[0] = same_ref[...].astype(jnp.float32)
    wide[1] = cross_ref[...].astype(jnp.float32)
    lane = lax.broadcasted_iota(jnp.int32, (GROUP, depth), 1)
    sub = lax.broadcasted_iota(jnp.int32, (GROUP, depth), 0)
    mask = (lane % GROUP == sub).astype(jnp.float32)[None]

    def one_pair(pair, carry):
        parts = []
        for h in range(2):
            g = 2 * pair + h
            left = []
            for place in range(2):
                line = wide[place, :, pl.ds(g, 1), :]
                spread = jnp.broadcast_to(line, (count, GROUP, depth)) * mask
                left.append(spread.reshape(count * GROUP, depth).astype(jnp.bfloat16))
            value = jnp.dot(
                jnp.concatenate(left, axis=1), weights[g], preferred_element_type=jnp.float32
            )
            parts.append(value.reshape(count, GROUP, 2 * LANES))
        both = jnp.concatenate(parts, axis=1).astype(jnp.bfloat16)
        at = pl.multiple_of(pair * 2 * GROUP, 2 * GROUP)
        stacked[:, pl.ds(at, 2 * GROUP), :] = both[..., :LANES]
        stacked[:, pl.ds(bins + at, 2 * GROUP), :] = both[..., LANES:]
        return carry

    lax.fori_loop(0, groups // 2, one_pair, 0)
    padded = (rows + 15) // 16 * 16

    def one_batch(index, carry):
        turned = [stacked[index * batch + i].T[:padded] for i in range(batch)]
        value = jnp.dot(
            jnp.concatenate(turned, axis=0), table_ref[...], preferred_element_type=jnp.float32
        )
        for i in range(batch):
            part = value[i * padded : i * padded + rows]
            out_ref[0, index * batch + i] = part.astype(jnp.bfloat16)
        return carry

    lax.fori_loop(0, count // batch, one_batch, 0)


def whole(shape):
    return pl.BlockSpec(shape, lambda i: (0,) * len(shape))


def local(signal, valid_flags):
    rows = signal.shape[0]
    windows = signal.shape[1] // WINDOW
    chan, tm = lax.axis_size("chan"), lax.axis_size("tm")
    groups = WINDOW // 2 // GROUP
    depth = 2 * windows * GROUP
    half_rows = rows // tm
    own = pl.pallas_call(
        spectra_kernel,
        out_shape=jax.ShapeDtypeStruct((groups, 2, windows * GROUP, LANES), jnp.bfloat16),
        scratch_shapes=[pltpu.VMEM((windows, LANES, WINDOW), jnp.bfloat16)],
        compiler_params=pltpu.CompilerParams(vmem_limit_bytes=VMEM_LIMIT),
    )(signal, valid_flags, taper_table(WINDOW), forward_table(WINDOW))
    own = own.reshape(groups, depth, LANES)
    lines = jnp.transpose(own, (2, 0, 1))
    me = lax.axis_index("tm")
    same_half = lax.dynamic_slice_in_dim(lines, me * half_rows, half_rows, 0)
    other_half = lax.dynamic_slice_in_dim(lines, (1 - me) * half_rows, half_rows, 0)
    other = lax.ppermute(own, "tm", [(0, 1), (1, 0)])
    table = lag_table(WINDOW, LAGS, windows * tm)
    received = []
    for r in range(ROUNDS):
        pair = []
        for value, flip in ((same_half, 0), (other_half, 1)):
            moves = [
                (b * tm + t, ((b - r - 1) % chan) * tm + (t ^ flip))
                for b in range(chan)
                for t in range(tm)
            ]
            pair.append(lax.ppermute(value, ("chan", "tm"), moves))
        received.append(pair)
    out_shape = (ROUNDS, half_rows, rows, LAGS)
    batch = next(n for n in (4, 2, 1) if half_rows % n == 0)
    out = None
    for r in range(ROUNDS):
        args = [own, other, *received[r], table]
        specs = [whole(a.shape) for a in args]
        aliases = {}
        if out is not None:
            args.append(out)
            specs.append(pl.BlockSpec(memory_space=pl.ANY))
            aliases = {len(args) - 1: 0}
        out = pl.pallas_call(
            functools.partial(cross_kernel, batch=batch),
            grid=(1,),
            in_specs=specs,
            out_specs=pl.BlockSpec((1, half_rows, rows, LAGS), lambda i, r=r: (r, 0, 0, 0)),
            out_shape=jax.ShapeDtypeStruct(out_shape, jnp.bfloat16),
            scratch_shapes=[
                pltpu.VMEM((groups, tm * depth, 2 * LANES), jnp.bfloat16),
                pltpu.VMEM((tm, half_rows, groups, depth), jnp.float32),
                pltpu.VMEM((half_rows, WINDOW, LANES), jnp.bfloat16),
            ],
            input_output_aliases=aliases,
            compiler_params=pltpu.CompilerParams(vmem_limit_bytes=VMEM_LIMIT),
            cost_estimate=pl.CostEstimate(
                flops=2 * half_rows * rows * WINDOW * LAGS * 2, bytes_accessed=10**7, transcendentals=0
            ),
        )(*args)
    return out


def solution(mesh):
    return jax.shard_map(
        local,
        mesh=mesh,
        in_specs=(P(("group", "chan"), "tm"), P(("group", "chan"), "tm")),
        out_specs=P(None, "tm", ("group", "chan"), None),
        check_vma=False,
    )
```

```python
import functools

import jax
import jax.numpy as jnp
import numpy as np
from jax import lax
from jax.experimental import pallas as pl
from jax.experimental.pallas import tpu as pltpu
from jax.sharding import PartitionSpec as P

WINDOW = 1024
LAGS = 512
ROUNDS = 2
EPSILON = 1e-06
GROUP = 8
LANES = 128
VMEM_LIMIT = 56 * 1024 * 1024
CROSS_LIMIT = 40 * 1024 * 1024


def taper_table(window):
    t = np.arange(window, dtype=np.float32)
    return (0.5 - 0.5 * np.cos(2.0 * np.pi * t / window)).astype(np.float32)[None, :]


def forward_table(window):
    bins = window // 2
    f = np.arange(bins, dtype=np.int64)[:, None]
    t = np.arange(window, dtype=np.int64)[None, :]
    phases = 2.0 * np.pi / window * (f * t % window)
    table = np.stack([np.cos(phases), -np.sin(phases)])
    table = table.reshape(2, bins // GROUP, GROUP, window).transpose(1, 0, 2, 3)
    return table.reshape(window, window).astype(jnp.bfloat16)


def lag_table(window, lag_count, windows):
    f = np.arange(window // 2, dtype=np.int64)[:, None]
    tau = np.arange(lag_count, dtype=np.int64)[None, :] - lag_count // 2
    phases = 2.0 * np.pi / window * (f * tau % window)
    weight = np.where(f == 0, 1.0, 2.0) / (window * float(window * windows) ** 0.5)
    return np.concatenate([weight * np.cos(phases), -weight * np.sin(phases)]).astype(jnp.bfloat16)


def spectra_kernel(signal_ref, flags_ref, taper_ref, table_ref, out_ref, *rest):
    send_refs, (tapered, lines) = rest[:-2], rest[-2:]
    rows = signal_ref.shape[0]
    windows = flags_ref.shape[0]
    groups, depth = out_ref.shape[:2]
    half = depth // 2
    flags = flags_ref[...].astype(jnp.float32).T
    tapered[:, rows:, :] = jnp.zeros((windows, LANES - rows, WINDOW), jnp.bfloat16)
    for w in range(windows):
        piece = signal_ref[:, w * WINDOW : (w + 1) * WINDOW]
        scale = lax.rsqrt(jnp.mean(piece * piece, axis=1, keepdims=True) + EPSILON)
        value = (piece * scale * taper_ref[...]) * flags[:, w : w + 1]
        tapered[w, :rows, :] = value.astype(jnp.bfloat16)
    for pair in range(windows // 2):
        two = tapered[2 * pair : 2 * pair + 2].reshape(2 * LANES, WINDOW)
        value = lax.dot_general(
            table_ref[...], two, (((1,), (1,)), ((), ())), preferred_element_type=jnp.float32
        )
        value = value.reshape(groups, 2, GROUP, 2 * LANES)
        value = jnp.concatenate([value[..., :LANES], value[..., LANES:]], axis=2)
        value = value.astype(jnp.bfloat16)
        at = pair * 2 * GROUP
        out_ref[:, at : at + 2 * GROUP, :] = value[:, 0]
        out_ref[:, half + at : half + at + 2 * GROUP, :] = value[:, 1]

    def one_group(g, carry):
        lines[pl.ds(g, LANES, stride=groups), :] = out_ref[g].T.astype(jnp.float32)
        return carry

    lax.fori_loop(0, groups, one_group, 0, unroll=4)
    me = lax.axis_index("tm")
    count = send_refs[0].shape[0]
    for index, ref in enumerate(send_refs):
        chunk, flip = index // 2, index % 2
        start = (me if flip == 0 else 1 - me) * (rows // 2) + chunk * count
        start = pl.multiple_of(start * groups, groups)
        value = lines[pl.ds(start, count * groups), :]
        ref[...] = value.astype(jnp.bfloat16).reshape(count, groups, depth)


def cross_kernel(own_ref, other_ref, same_ref, cross_ref, table_ref, *rest, batch):
    out_ref, wide, stacked = rest[-3:]
    count = same_ref.shape[0]
    rows = out_ref.shape[2]
    groups, depth = own_ref.shape[:2]
    half = depth // 2
    bins = groups * GROUP
    wide[0] = same_ref[...].astype(jnp.float32)
    wide[1] = cross_ref[...].astype(jnp.float32)
    lane = lax.broadcasted_iota(jnp.int32, (GROUP, depth), 1)
    sub = lax.broadcasted_iota(jnp.int32, (GROUP, depth), 0)
    mask = (lane % GROUP == sub).astype(jnp.float32)[None]

    def one_pair(pair, carry):
        parts = []
        for h in range(2):
            g = 2 * pair + h
            left, real, imag = [], [], []
            for place, ref in enumerate((own_ref, other_ref)):
                line = wide[place, :, pl.ds(g, 1), :]
                spread = jnp.broadcast_to(line, (count, GROUP, depth)) * mask
                left.append(spread.reshape(count * GROUP, depth).astype(jnp.bfloat16))
                block = ref[g]
                real.append(block)
                imag += [block[half:], -block[:half]]
            weights = jnp.concatenate(
                [jnp.concatenate(real, axis=0), jnp.concatenate(imag, axis=0)], axis=1
            )
            value = jnp.dot(
                jnp.concatenate(left, axis=1), weights, preferred_element_type=jnp.float32
            )
            parts.append(value.reshape(count, GROUP, 2 * LANES))
        both = jnp.concatenate(parts, axis=1).astype(jnp.bfloat16)
        at = pl.multiple_of(pair * 2 * GROUP, 2 * GROUP)
        stacked[:, pl.ds(at, 2 * GROUP), :] = both[..., :LANES]
        stacked[:, pl.ds(bins + at, 2 * GROUP), :] = both[..., LANES:]
        return carry

    lax.fori_loop(0, groups // 2, one_pair, 0, unroll=2)
    padded = (rows + 15) // 16 * 16

    def one_batch(index, carry):
        turned = [stacked[index * batch + i].T[:padded] for i in range(batch)]
        value = jnp.dot(
            jnp.concatenate(turned, axis=0), table_ref[...], preferred_element_type=jnp.float32
        )
        for i in range(batch):
            part = value[i * padded : i * padded + rows]
            out_ref[0, index * batch + i] = part.astype(jnp.bfloat16)
        return carry

    lax.fori_loop(0, count // batch, one_batch, 0)


def whole(shape):
    return pl.BlockSpec(shape, lambda i: (0,) * len(shape))


def local(signal, valid_flags):
    rows = signal.shape[0]
    windows = signal.shape[1] // WINDOW
    chan, tm = lax.axis_size("chan"), lax.axis_size("tm")
    groups = WINDOW // 2 // GROUP
    depth = 2 * windows * GROUP
    half_rows = rows // tm
    chunks = 2 if half_rows % 2 == 0 else 1
    count = half_rows // chunks
    piece = jax.ShapeDtypeStruct((count, groups, depth), jnp.bfloat16)
    own, *sends = pl.pallas_call(
        spectra_kernel,
        out_shape=[jax.ShapeDtypeStruct((groups, depth, LANES), jnp.bfloat16)]
        + [piece] * (2 * chunks),
        scratch_shapes=[
            pltpu.VMEM((windows, LANES, WINDOW), jnp.bfloat16),
            pltpu.VMEM((LANES * groups, depth), jnp.float32),
        ],
        compiler_params=pltpu.CompilerParams(vmem_limit_bytes=VMEM_LIMIT),
    )(signal, valid_flags.T, taper_table(WINDOW), forward_table(WINDOW))
    table = lag_table(WINDOW, LAGS, windows * tm)

    def moved(value, steps, flip):
        moves = [
            (b * tm + t, ((b - steps) % chan) * tm + (t ^ flip))
            for b in range(chan)
            for t in range(tm)
        ]
        return lax.ppermute(value, ("chan", "tm"), moves)

    def chosen(q, flip, handed):
        if chan % 2:
            return sends[2 * q + flip]
        return jnp.where(lax.axis_index("chan") % 2 == 1, sends[2 * q + flip], handed)

    def paired(value, flip):
        if chan % 2:
            return moved(value, 1, flip)
        moves = [
            (b * tm + t, (b ^ 1) * tm + (t ^ (flip if b % 2 else 0)))
            for b in range(chan)
            for t in range(tm)
        ]
        return lax.ppermute(value, ("chan", "tm"), moves)

    received = {}
    other = None
    for q in range(chunks):
        for flip in range(2):
            received[1, q, flip] = moved(sends[2 * q + flip], 2, flip)
        if other is None:
            other = lax.ppermute(own, "tm", [(0, 1), (1, 0)])
    out_shape = (ROUNDS, half_rows, rows, LAGS)
    batch = next(n for n in (13, 8, 7, 5, 4, 3, 2, 1) if count % n == 0)

    def cross(out, r, q):
        args = [own, other, received[r, q, 0], received[r, q, 1], table]
        specs = [whole(a.shape) for a in args]
        aliases = {}
        if out is not None:
            args.append(out)
            specs.append(pl.BlockSpec(memory_space=pl.ANY))
            aliases = {len(args) - 1: 0}
        return pl.pallas_call(
            functools.partial(cross_kernel, batch=batch),
            grid=(1,),
            in_specs=specs,
            out_specs=pl.BlockSpec((1, count, rows, LAGS), lambda i, r=r, q=q: (r, q, 0, 0)),
            out_shape=jax.ShapeDtypeStruct(out_shape, jnp.bfloat16),
            scratch_shapes=[
                pltpu.VMEM((tm, count, groups, depth), jnp.float32),
                pltpu.VMEM((count, WINDOW, LANES), jnp.bfloat16),
            ],
            input_output_aliases=aliases,
            compiler_params=pltpu.CompilerParams(vmem_limit_bytes=CROSS_LIMIT),
            cost_estimate=pl.CostEstimate(
                flops=10**10, bytes_accessed=10**7, transcendentals=0
            ),
        )(*args)

    for flip in range(2):
        received[0, 0, flip] = paired(chosen(0, flip, received[1, 0, flip]), flip)
    out = cross(None, 1, 0)
    for q in range(1, chunks):
        came = [received[1, q, flip] for flip in range(2)]
        out, *came = lax.optimization_barrier((out, *came))
        values = [chosen(q, flip, came[flip]) for flip in range(2)]
        out, *values = lax.optimization_barrier((out, *values))
        for flip in range(2):
            received[0, q, flip] = paired(values[flip], flip)
        out = cross(out, 1, q)
        out = cross(out, 0, q - 1)
    return cross(out, 0, chunks - 1)


def solution(mesh):
    return jax.shard_map(
        local,
        mesh=mesh,
        in_specs=(P(("group", "chan"), "tm"), P(("group", "chan"), "tm")),
        out_specs=P(None, "tm", ("group", "chan"), None),
        check_vma=False,
    )
```

```python
import functools

import jax
import jax.numpy as jnp
import numpy as np
from jax import lax
from jax.experimental import pallas as pl
from jax.experimental.pallas import tpu as pltpu
from jax.sharding import PartitionSpec as P

WINDOW = 1024
LAGS = 512
ROUNDS = 2
EPSILON = 1e-06
GROUP = 8
LANES = 128
VMEM_LIMIT = 56 * 1024 * 1024
CROSS_LIMIT = 32 * 1024 * 1024


def taper_table(window):
    t = np.arange(window, dtype=np.float32)
    return (0.5 - 0.5 * np.cos(2.0 * np.pi * t / window)).astype(np.float32)[None, :]


def forward_table(window):
    bins = window // 2
    f = np.arange(bins, dtype=np.int64)[:, None]
    t = np.arange(window, dtype=np.int64)[None, :]
    phases = 2.0 * np.pi / window * (f * t % window)
    table = np.stack([np.cos(phases), -np.sin(phases)])
    table = table.reshape(2, bins // GROUP, GROUP, window).transpose(1, 0, 2, 3)
    return table.reshape(window, window).astype(jnp.bfloat16)


def lag_table(window, lag_count, windows):
    f = np.arange(window // 2, dtype=np.int64)[:, None]
    tau = np.arange(lag_count, dtype=np.int64)[None, :] - lag_count // 2
    phases = 2.0 * np.pi / window * (f * tau % window)
    weight = np.where(f == 0, 1.0, 2.0) / (window * float(window * windows) ** 0.5)
    return np.concatenate([weight * np.cos(phases), -weight * np.sin(phases)]).astype(jnp.bfloat16)


def spectra_kernel(signal_ref, flags_ref, taper_ref, table_ref, out_ref, *rest):
    send_refs, (tapered, lines) = rest[:-2], rest[-2:]
    rows = signal_ref.shape[0]
    windows = flags_ref.shape[0]
    groups, depth = out_ref.shape[:2]
    half = depth // 2
    flags = flags_ref[...].astype(jnp.float32).T
    tapered[:, rows:, :] = jnp.zeros((windows, LANES - rows, WINDOW), jnp.bfloat16)
    for w in range(windows):
        piece = signal_ref[:, w * WINDOW : (w + 1) * WINDOW]
        scale = lax.rsqrt(jnp.mean(piece * piece, axis=1, keepdims=True) + EPSILON)
        value = (piece * scale * taper_ref[...]) * flags[:, w : w + 1]
        tapered[w, :rows, :] = value.astype(jnp.bfloat16)
    for pair in range(windows // 2):
        two = tapered[2 * pair : 2 * pair + 2].reshape(2 * LANES, WINDOW)
        value = lax.dot_general(
            table_ref[...], two, (((1,), (1,)), ((), ())), preferred_element_type=jnp.float32
        )
        value = value.reshape(groups, 2, GROUP, 2 * LANES)
        value = jnp.concatenate([value[..., :LANES], value[..., LANES:]], axis=2)
        value = value.astype(jnp.bfloat16)
        at = pair * 2 * GROUP
        out_ref[:, at : at + 2 * GROUP, :] = value[:, 0]
        out_ref[:, half + at : half + at + 2 * GROUP, :] = value[:, 1]

    def one_group(g, carry):
        lines[pl.ds(g, LANES, stride=groups), :] = out_ref[g].T.astype(jnp.float32)
        return carry

    lax.fori_loop(0, groups, one_group, 0, unroll=16)
    me = lax.axis_index("tm")
    count = send_refs[0].shape[0]
    for index, ref in enumerate(send_refs):
        chunk, flip = index // 2, index % 2
        start = (me if flip == 0 else 1 - me) * (rows // 2) + chunk * count
        start = pl.multiple_of(start * groups, groups)
        value = lines[pl.ds(start, count * groups), :]
        ref[...] = value.astype(jnp.bfloat16).reshape(count, groups, depth)


def cross_kernel(own_ref, other_ref, same_ref, cross_ref, table_ref, *rest, batch):
    out_ref, wide, stacked = rest[-3:]
    count = same_ref.shape[0]
    rows = out_ref.shape[2]
    groups, depth = own_ref.shape[:2]
    half = depth // 2
    bins = groups * GROUP
    wide[0] = same_ref[...].astype(jnp.float32)
    wide[1] = cross_ref[...].astype(jnp.float32)
    lane = lax.broadcasted_iota(jnp.int32, (GROUP, depth), 1)
    sub = lax.broadcasted_iota(jnp.int32, (GROUP, depth), 0)
    mask = (lane % GROUP == sub).astype(jnp.float32)[None]

    def one_pair(pair, carry):
        parts = []
        for h in range(2):
            g = 2 * pair + h
            left, real, imag = [], [], []
            for place, ref in enumerate((own_ref, other_ref)):
                line = wide[place, :, pl.ds(g, 1), :]
                spread = jnp.broadcast_to(line, (count, GROUP, depth)) * mask
                left.append(spread.reshape(count * GROUP, depth).astype(jnp.bfloat16))
                block = ref[g]
                real.append(block)
                imag += [block[half:], -block[:half]]
            weights = jnp.concatenate(
                [jnp.concatenate(real, axis=0), jnp.concatenate(imag, axis=0)], axis=1
            )
            value = jnp.dot(
                jnp.concatenate(left, axis=1), weights, preferred_element_type=jnp.float32
            )
            parts.append(value.reshape(count, GROUP, 2 * LANES))
        both = jnp.concatenate(parts, axis=1).astype(jnp.bfloat16)
        at = pl.multiple_of(pair * 2 * GROUP, 2 * GROUP)
        stacked[:, pl.ds(at, 2 * GROUP), :] = both[..., :LANES]
        stacked[:, pl.ds(bins + at, 2 * GROUP), :] = both[..., LANES:]
        return carry

    lax.fori_loop(0, groups // 2, one_pair, 0, unroll=8)
    padded = (rows + 15) // 16 * 16

    def one_batch(index, carry):
        turned = [stacked[index * batch + i].T[:padded] for i in range(batch)]
        value = jnp.dot(
            jnp.concatenate(turned, axis=0), table_ref[...], preferred_element_type=jnp.float32
        )
        for i in range(batch):
            part = value[i * padded : i * padded + rows]
            out_ref[0, index * batch + i] = part.astype(jnp.bfloat16)
        return carry

    lax.fori_loop(0, count // batch, one_batch, 0)


def local(signal, valid_flags):
    rows = signal.shape[0]
    windows = signal.shape[1] // WINDOW
    chan, tm = lax.axis_size("chan"), lax.axis_size("tm")
    groups = WINDOW // 2 // GROUP
    depth = 2 * windows * GROUP
    half_rows = rows // tm
    chunks = 2 if half_rows % 2 == 0 else 1
    count = half_rows // chunks
    piece = jax.ShapeDtypeStruct((count, groups, depth), jnp.bfloat16)
    own, *sends = pl.pallas_call(
        spectra_kernel,
        out_shape=[jax.ShapeDtypeStruct((groups, depth, LANES), jnp.bfloat16)]
        + [piece] * (2 * chunks),
        scratch_shapes=[
            pltpu.VMEM((windows, LANES, WINDOW), jnp.bfloat16),
            pltpu.VMEM((LANES * groups, depth), jnp.float32),
        ],
        compiler_params=pltpu.CompilerParams(vmem_limit_bytes=VMEM_LIMIT),
    )(signal, valid_flags.T, taper_table(WINDOW), forward_table(WINDOW))
    table = lag_table(WINDOW, LAGS, windows * tm)

    def moved(value, steps, flip):
        moves = [
            (b * tm + t, ((b - steps) % chan) * tm + (t ^ flip))
            for b in range(chan)
            for t in range(tm)
        ]
        return lax.ppermute(value, ("chan", "tm"), moves)

    def chosen(q, flip, handed):
        if chan % 2:
            return sends[2 * q + flip]
        return jnp.where(lax.axis_index("chan") % 2 == 1, sends[2 * q + flip], handed)

    def paired(value, flip):
        if chan % 2:
            return moved(value, 1, flip)
        moves = [
            (b * tm + t, (b ^ 1) * tm + (t ^ (flip if b % 2 else 0)))
            for b in range(chan)
            for t in range(tm)
        ]
        return lax.ppermute(value, ("chan", "tm"), moves)

    received = {}
    other = None
    for q in range(chunks):
        for flip in range(2):
            received[1, q, flip] = moved(sends[2 * q + flip], 2, flip)
        if other is None:
            other = lax.ppermute(own, "tm", [(0, 1), (1, 0)])
    out_shape = (ROUNDS, half_rows, rows, LAGS)
    batch = next(n for n in (13, 8, 7, 5, 4, 3, 2, 1) if count % n == 0)

    def cross(out, r, q):
        args = [own, other, received[r, q, 0], received[r, q, 1], table]
        specs = [pl.BlockSpec(memory_space=pltpu.VMEM) for _ in args]
        aliases = {}
        if out is not None:
            args.append(out)
            specs.append(pl.BlockSpec(memory_space=pl.ANY))
            aliases = {len(args) - 1: 0}
        return pl.pallas_call(
            functools.partial(cross_kernel, batch=batch),
            grid=(1,),
            in_specs=specs,
            out_specs=pl.BlockSpec((1, count, rows, LAGS), lambda i, r=r, q=q: (r, q, 0, 0)),
            out_shape=jax.ShapeDtypeStruct(out_shape, jnp.bfloat16),
            scratch_shapes=[
                pltpu.VMEM((tm, count, groups, depth), jnp.float32),
                pltpu.VMEM((count, WINDOW, LANES), jnp.bfloat16),
            ],
            input_output_aliases=aliases,
            compiler_params=pltpu.CompilerParams(vmem_limit_bytes=CROSS_LIMIT),
            cost_estimate=pl.CostEstimate(
                flops=10**10, bytes_accessed=10**7, transcendentals=0
            ),
        )(*args)

    for flip in range(2):
        received[0, 0, flip] = paired(chosen(0, flip, received[1, 0, flip]), flip)
    out = cross(None, 1, 0)
    for q in range(1, chunks):
        came = [received[1, q, flip] for flip in range(2)]
        out, *came = lax.optimization_barrier((out, *came))
        values = [chosen(q, flip, came[flip]) for flip in range(2)]
        out, *values = lax.optimization_barrier((out, *values))
        for flip in range(2):
            received[0, q, flip] = paired(values[flip], flip)
        out = cross(out, 1, q)
        out = cross(out, 0, q - 1)
    return cross(out, 0, chunks - 1)


def solution(mesh):
    return jax.shard_map(
        local,
        mesh=mesh,
        in_specs=(P(("group", "chan"), "tm"), P(("group", "chan"), "tm")),
        out_specs=P(None, "tm", ("group", "chan"), None),
        check_vma=False,
    )
```
